32 devices in a mesh: seq: 8 (over z, x), head: 4 (over y, core).
Axes of the slice: x: 2, y: 2, z: 4, core: 2. Of those that a mesh axis runs over, the one named last changes fastest.
Arguments:
- values: bfloat16 [24, 64, 32768], P('head', None, 'seq'), may hold values from -6 to 6
- b_rows: bfloat16 [128, 32768], P(None, ('seq', 'head')), may hold values from -0.59765625 to 0.59765625
- c_rows: bfloat16 [128, 32768], P(None, ('seq', 'head')), may hold values from -0.59765625 to 0.59765625
- log_decay: float32 [24, 32768], P('head', 'seq'), may hold values from -0.6 to 0
- level_weight: float32 [10, 24, 32768], P(None, 'head', 'seq'), may hold values from 0 to 2
Outputs:
- layer_out: bfloat16 [24, 64, 32768], P('head', None, 'seq')
The draws below stay inside these ranges and needn't reach their ends.
All inputs are finite; a program needn't handle non-finite values.
Results may differ from the reference program's by a relative error of at most 0.0034.
Values may be sent and summed in bfloat16 or wider, within the bound.
A program may use at most 128 MiB of HBM per device.

```python
import math
import jax
import jax.numpy as jnp
from jax import lax

HEAD_TOTAL = 24
STATE = 128
HEAD_DIM = 64
STRETCH = 64
TOKEN_TOTAL = 32768
LEVELS = 10


def draw_log_decay(key, part):
    key = jax.random.fold_in(key, 11)
    key_sequence = jax.random.split(key, 6)
    slow_share = 0.5
    slow_mask = jax.random.bernoulli(key_sequence[0], slow_share, (HEAD_TOTAL, 1))
    slow_rate = 0.25 * math.log(10.0) / TOKEN_TOTAL
    fast_rate = jnp.exp(jax.random.uniform(key_sequence[1], (HEAD_TOTAL, 1), jnp.float32, math.log(1.0 / 50.0), math.log(1.0 / 30.0)))
    baseline_rate = jnp.where(slow_mask, slow_rate, fast_rate)
    block_multiplier = jnp.repeat(jax.random.uniform(key_sequence[2], (HEAD_TOTAL, TOKEN_TOTAL // STRETCH), jnp.float32, 0.5, 1.5), STRETCH, axis=1)
    jaggedness = jax.random.uniform(key_sequence[3], (HEAD_TOTAL, TOKEN_TOTAL), jnp.float32, 0.4, 1.6)
    spike_mask = jax.random.bernoulli(key_sequence[4], 3.0 / TOKEN_TOTAL, (HEAD_TOTAL, TOKEN_TOTAL))
    spike_length = jax.random.uniform(key_sequence[5], (HEAD_TOTAL, TOKEN_TOTAL), jnp.float32, 0.22, 0.5)
    return -(baseline_rate * block_multiplier * jaggedness + jnp.where(spike_mask, spike_length, 0.0))


def draw_level_weight(key, part):
    key = jax.random.fold_in(key, 23)
    base_draw = jnp.exp(jax.random.uniform(key, (LEVELS, HEAD_TOTAL, TOKEN_TOTAL), jnp.float32, math.log(0.5), math.log(2.0)))
    level_ids = jnp.arange(LEVELS).astype(jnp.float32)
    level_scale = jnp.exp2(-0.5 * jnp.maximum(level_ids - 1.0, 0.0))
    return level_scale[:, None, None] * base_draw


def block_levels(key, extent, pieces, low, largest):
    def one(axis_at, parts):
        heights = jax.random.uniform(jax.random.fold_in(jax.random.fold_in(key, 6), axis_at), (parts,), jnp.float32, low / len(pieces), largest / len(pieces))
        return jnp.repeat(jnp.exp(heights), extent[axis_at] // parts).reshape((-1,) + (1,) * (len(extent) - axis_at - 1))

    gain = one(*pieces[0])
    for cut in pieces[1:]:
        gain = gain * one(*cut)
    return gain


def gaussian(stream_key, dims, deviation, most, cuts=(), dtype=jnp.bfloat16):
    factor_of = block_levels(stream_key, dims, cuts, -0.22, 0.18) if cuts else 1.0
    values = jax.random.normal(stream_key, dims, jnp.float32) * deviation * factor_of
    return jnp.minimum(jnp.maximum(values, -most), most).astype(dtype)


def setup_inputs(seed: int = 0) -> dict:
    arg_keys = jax.random.split(jax.random.key(seed), 6)
    values = gaussian(arg_keys[0], (HEAD_TOTAL, HEAD_DIM, TOKEN_TOTAL), 1.0, 6.0, ((0, 4), (2, 8)))
    b_rows = gaussian(arg_keys[1], (STATE, TOKEN_TOTAL), 0.1, 0.59765625, ((1, 32),))
    c_rows = gaussian(arg_keys[2], (STATE, TOKEN_TOTAL), 0.1, 0.59765625, ((1, 32),))
    log_decay = draw_log_decay(jax.random.fold_in(arg_keys[5], 71), 0)
    level_weight = draw_level_weight(jax.random.fold_in(arg_keys[5], 71), 0)
    return {"values": values, "b_rows": b_rows, "c_rows": c_rows, "log_decay": log_decay, "level_weight": level_weight}


def reference(values, b_rows, c_rows, log_decay, level_weight):
    stretch_count = TOKEN_TOTAL // STRETCH
    b_blk = b_rows.astype(jnp.float32).reshape(STATE, stretch_count, STRETCH)
    c_blk = c_rows.astype(jnp.float32).reshape(STATE, stretch_count, STRETCH)
    scores = jnp.einsum('nkt,nks->kts', c_blk, b_blk, precision=lax.Precision.HIGHEST)
    causal = jnp.arange(STRETCH)[:, None] >= jnp.arange(STRETCH)[None, :]
    weights_t = jnp.transpose(level_weight, (1, 0, 2))

    def one_head(packed):
        head_vals, head_decay, head_weight = packed
        val_blk = head_vals.astype(jnp.float32).reshape(HEAD_DIM, stretch_count, STRETCH)
        cum_log = jnp.cumsum(head_decay.reshape(stretch_count, STRETCH), axis=1)
        stretch_tot = cum_log[:, -1]
        diff_log = cum_log[:, :, None] - cum_log[:, None, :]
        decay = jnp.exp(jnp.where(causal[None], diff_log, -jnp.inf))
        weight_zero = head_weight[0].reshape(stretch_count, STRETCH)
        mix = (weight_zero[:, :, None] * decay * scores).astype(jnp.bfloat16)
        result = jnp.einsum('kts,pks->pkt', mix.astype(jnp.float32), val_blk, precision=lax.Precision.HIGHEST)
        keys_decayed = (jnp.exp(stretch_tot[:, None] - cum_log)[None] * b_blk).astype(jnp.bfloat16)
        state = jnp.einsum('nks,pks->knp', keys_decayed.astype(jnp.float32), val_blk, precision=lax.Precision.HIGHEST)
        c_exp = jnp.exp(cum_log)[None] * c_blk
        agg, tot_blk = state, stretch_tot
        for level in range(LEVELS - 1):
            span = 2 ** level
            groups = stretch_count // (2 * span)
            paired = agg.reshape(groups, 2, STATE, HEAD_DIM)
            left_part = paired[:, 0]
            right_part = paired[:, 1]
            tot_pair = tot_blk.reshape(groups, 2)
            src_tot = stretch_tot.reshape(groups, 2, span)[:, 1]
            pre_tot = jnp.concatenate([jnp.zeros((groups, 1), jnp.float32), jnp.cumsum(src_tot[:, :-1], axis=1)], axis=1)
            carried = jnp.exp(pre_tot)[:, :, None, None] * left_part[:, None]
            c_right = c_exp.reshape(STATE, groups, 2, span, STRETCH)[:, :, 1]
            w_right = head_weight[level + 1].reshape(groups, 2, span, STRETCH)[:, 1]
            contrib = jnp.einsum('ngwq,gwnp->pgwq', c_right, carried, precision=lax.Precision.HIGHEST) * w_right[None]
            result = result.reshape(HEAD_DIM, groups, 2, span, STRETCH).at[:, :, 1].add(contrib).reshape(HEAD_DIM, stretch_count, STRETCH)
            agg = jnp.exp(tot_pair[:, 1])[:, None, None] * left_part + right_part
            tot_blk = tot_pair[:, 0] + tot_pair[:, 1]
        return result.reshape(HEAD_DIM, TOKEN_TOTAL).astype(jnp.bfloat16)

    return lax.map(one_head, (values, log_decay, weights_t))
```

```python
import functools

import jax
import jax.numpy as jnp
from jax import lax
from jax.experimental import pallas as pl
from jax.experimental.pallas import tpu as pltpu
from jax.sharding import PartitionSpec as P

STRETCH = 64
BLOCK = 256
HALF = BLOCK // 2
LANES = 128
ROWS = 8
MESH = pl.DeviceIdType.MESH
F32 = jnp.float32
BF16 = jnp.bfloat16


def flip(index, bit):
    return index + bit * (1 - 2 * lax.rem(lax.div(index, bit), 2))


def flip_all(index, mask):
    bit = 1
    while bit <= mask:
        if mask & bit:
            index = flip(index, bit)
        bit *= 2
    return index


def bits_down(count):
    bit = count // 2
    while bit:
        yield bit
        bit //= 2


def exchange_kernel(
    head_devices,
    seq_devices,
    v_hbm,
    b_hbm,
    c_hbm,
    ld_ref,
    b_all,
    c_all,
    lefts,
    dev_states,
    dev_offs,
    cum_ref,
    v_vmem,
    steps_ref,
    states,
    tots,
    group,
    send_state,
    send_tot,
    recv_tot,
    local_sem,
    gather_send,
    gather_recv,
    state_send,
    state_recv,
    tot_send,
    tot_recv,
):
    heads, width, rows = v_hbm.shape
    cols = b_hbm.shape[1]
    blocks = rows // BLOCK
    seq_bits = seq_devices.bit_length() - 1
    me = lax.axis_index("head")
    seq = lax.axis_index("seq")

    load_v = pltpu.make_async_copy(v_hbm, v_vmem, local_sem.at[0])
    load_v.start()

    partners = [("head", flip(me, bit)) for bit in bits_down(head_devices)]
    partners += [("seq", flip(seq, 2**q)) for q in range(seq_bits)]
    barrier = pltpu.get_barrier_semaphore()
    for axis, who in partners:
        pl.semaphore_signal(barrier, inc=1, device_id={axis: who}, device_id_type=MESH)
    pl.semaphore_wait(barrier, len(partners))

    def slot(full, owner):
        return full.at[:, pl.ds(pl.multiple_of(owner * cols, cols), cols)]

    pairs = ((b_hbm, b_all), (c_hbm, c_all))

    def message(a, mask):
        shard, full = pairs[a]
        bit = mask & -mask
        held = mask ^ bit
        owner = flip_all(me, held)
        return pltpu.make_async_remote_copy(
            src_ref=slot(full, owner) if held else shard,
            dst_ref=slot(full, owner),
            send_sem=gather_send.at[a, mask],
            recv_sem=gather_recv.at[a, mask],
            device_id={"head": flip(me, bit)},
            device_id_type=MESH,
        )

    def send_own(a):
        for bit in bits_down(head_devices):
            message(a, bit).start()

    def collect(a):
        for bit in bits_down(head_devices):
            for mask in range(bit, head_devices, 2 * bit):
                message(a, mask).wait_recv()
                for lower in bits_down(bit):
                    message(a, mask | lower).start()

    send_own(0)
    send_own(1)
    own = []
    for a, (shard, full) in enumerate(pairs):
        copy = pltpu.make_async_copy(shard, slot(full, me), local_sem.at[1 + a])
        copy.start()
        own.append(copy)

    steps_ref[...] = jnp.zeros_like(steps_ref)
    for j in range(blocks):
        steps_ref[pl.ds(ROWS * j, heads), :] = ld_ref[:, pl.ds(BLOCK * j, BLOCK)]
    tri = (
        lax.broadcasted_iota(jnp.int32, (BLOCK, BLOCK), 0)
        <= lax.broadcasted_iota(jnp.int32, (BLOCK, BLOCK), 1)
    ).astype(F32)
    cum_ref[...] = jnp.dot(
        steps_ref[...], tri, precision=lax.Precision.HIGHEST, preferred_element_type=F32
    )

    load_v.wait()
    own[0].wait()
    collect(0)

    def block_state(j, carry):
        cum = cum_ref[pl.ds(pl.multiple_of(ROWS * j, ROWS), ROWS), :]
        total = cum[:, BLOCK - 1 : BLOCK]
        tots[j] = jnp.broadcast_to(total, (ROWS, LANES))
        fade = jnp.exp(total - cum)
        at = pl.ds(pl.multiple_of(BLOCK * j, BLOCK), BLOCK)
        faded = [
            (v_vmem[h, :, at].astype(F32) * fade[h : h + 1, :]).astype(BF16) for h in range(heads)
        ]
        states[j] = lax.dot_general(
            jnp.concatenate(faded, axis=0),
            b_all[:, at],
            (((1,), (1,)), ((), ())),
            preferred_element_type=F32,
        )
        return carry

    lax.fori_loop(0, blocks, block_state, 0)

    base = 0
    span = 1
    while span < blocks:
        groups = blocks // (2 * span)

        def merge(i, carry, span=span, base=base):
            left = i * (2 * span) + (span - 1)
            right = left + span
            lefts[base + i] = states[left].astype(BF16)
            fade = jnp.exp(tots[right])
            for h in range(heads):
                part = pl.ds(h * width, width)
                states[right, part, :] = (
                    fade[h : h + 1, :] * states[left, part, :] + states[right, part, :]
                )
            tots[right] = tots[left] + tots[right]
            return carry

        lax.fori_loop(0, groups, merge, 0)
        base += groups
        span *= 2

    last = blocks - 1
    my_tot = tots[last]
    off = jnp.zeros((ROWS, LANES), F32)
    group[...] = states[last]
    for q in range(seq_bits):
        partner = flip(seq, 2**q)
        right = lax.rem(lax.div(seq, 2**q), 2) == 1
        send_state[q] = group[...].astype(BF16)
        send_tot[q] = my_tot
        state_copy = pltpu.make_async_remote_copy(
            src_ref=send_state.at[q],
            dst_ref=dev_states.at[q],
            send_sem=state_send.at[q],
            recv_sem=state_recv.at[q],
            device_id={"seq": partner},
            device_id_type=MESH,
        )
        tot_copy = pltpu.make_async_remote_copy(
            src_ref=send_tot.at[q],
            dst_ref=recv_tot.at[q],
            send_sem=tot_send.at[q],
            recv_sem=tot_recv.at[q],
            device_id={"seq": partner},
            device_id_type=MESH,
        )
        tot_copy.start()
        state_copy.start()
        dev_offs[q] = off
        if q == min(1, seq_bits - 1):
            own[1].wait()
            collect(1)
        tot_copy.wait()
        state_copy.wait()
        if q < seq_bits - 1:
            other = recv_tot[q]
            mine_by = jnp.where(right, 1.0, jnp.exp(other))
            other_by = jnp.where(right, jnp.exp(my_tot), 1.0)
            for h in range(heads):
                part = pl.ds(h * width, width)
                group[part, :] = mine_by[h : h + 1, :] * group[part, :] + other_by[
                    h : h + 1, :
                ] * dev_states[q, part, :].astype(F32)
            off = off + jnp.where(right, other, 0.0)
            my_tot = my_tot + other

    for a in range(2):
        for mask in range(1, head_devices):
            message(a, mask).wait_send()


def output_kernel(
    seq_bits, v_ref, b_ref, c_ref, w_ref, cum_ref, *rest
):
    heads, width, _ = v_ref.shape
    local_bits = len(rest) - 5
    left_refs = rest[:local_bits]
    dev_states, dev_offs, out_ref, acc, run = rest[local_bits:]
    j = pl.program_id(0)
    seq = lax.axis_index("seq")

    @pl.when(j == 0)
    def _():
        run[...] = jnp.zeros_like(run)

    cum = cum_ref[...]
    c_blk = c_ref[...]
    scores = lax.dot_general(
        b_ref[...], c_blk, (((0,), (0,)), ((), ())), preferred_element_type=F32
    )
    s_at = lax.broadcasted_iota(jnp.int32, (BLOCK, BLOCK), 0)
    t_at = lax.broadcasted_iota(jnp.int32, (BLOCK, BLOCK), 1)
    scores = jnp.where(s_at <= t_at, scores, 0.0)

    lane = lax.broadcasted_iota(jnp.int32, (ROWS, BLOCK), 1)
    mid0 = cum[:, STRETCH - 1 : STRETCH]
    mid1 = cum[:, HALF + STRETCH - 1 : HALF + STRETCH]
    cut = cum[:, HALF - 1 : HALF]
    away = cum - jnp.where(lane < HALF, mid0, mid1)
    col = jnp.exp(-away).T
    col_cut = jnp.exp(cut - cum[:, :HALF]).T
    row = jnp.exp(away)[:heads]
    w0, w1, w2 = w_ref[0], w_ref[1], w_ref[2]
    near = (lax.broadcasted_iota(jnp.int32, (heads, BLOCK), 1) & STRETCH) == 0
    row_first = jnp.where(near, w0, w1) * row
    row_second = w0 * row
    row_cut = w2[:, HALF:] * jnp.exp(cum[:, HALF:] - cut)[:heads]

    def piece(h, s0, t0, col_part, row_part):
        size = col_part.shape[0]
        return (
            scores[s0 : s0 + size, t0 : t0 + HALF] * (col_part[:, h : h + 1] * row_part[h : h + 1, :])
        ).astype(BF16)

    empty = jnp.zeros((HALF, HALF), BF16)
    for h in range(heads):
        first = jnp.concatenate(
            [
                piece(h, 0, 0, col[:STRETCH], row_first[:, :HALF]),
                piece(h, STRETCH, 0, col[STRETCH:HALF], row_second[:, :HALF]),
                empty,
            ],
            axis=0,
        )
        second = jnp.concatenate(
            [
                piece(h, 0, HALF, col_cut, row_cut),
                piece(h, HALF, HALF, col[HALF : HALF + STRETCH], row_first[:, HALF:]),
                piece(h, HALF + STRETCH, HALF, col[HALF + STRETCH :], row_second[:, HALF:]),
            ],
            axis=0,
        )
        mix = jnp.concatenate([first, second], axis=1)
        acc[pl.ds(h * width, width), :] = jnp.dot(v_ref[h], mix, preferred_element_type=F32)

    def add_level(level, state, off):
        reads = jnp.dot(state, c_blk, preferred_element_type=F32)
        by = w_ref[level] * jnp.exp(cum + off[:, :1])[:heads]
        for h in range(heads):
            part = slice(h * width, (h + 1) * width)
            acc[part, :] += reads[part, :] * by[h : h + 1, :]

    for r in range(local_bits):

        @pl.when((j >> r) & 1 == 1)
        def _(r=r):
            add_level(3 + r, left_refs[r][0], run[r])

    for q in range(seq_bits):

        @pl.when((seq >> q) & 1 == 1)
        def _(q=q):
            add_level(3 + local_bits + q, dev_states[q], run[local_bits] + dev_offs[q])

    total = jnp.broadcast_to(cum[:, BLOCK - 1 : BLOCK], (ROWS, LANES))
    for r in range(local_bits):
        run[r] = jnp.where((j + 1) & (2**r - 1) == 0, 0.0, run[r] + total)
    run[local_bits] = run[local_bits] + total
    for h in range(heads):
        out_ref[h] = acc[pl.ds(h * width, width), :].astype(BF16)


def on_device(head_devices, seq_devices, values, b_rows, c_rows, log_decay, level_weight):
    heads, width, rows = values.shape
    state_size = b_rows.shape[0]
    blocks = rows // BLOCK
    local_bits = blocks.bit_length() - 1
    seq_bits = seq_devices.bit_length() - 1
    hp = heads * width
    hbm = pl.BlockSpec(memory_space=pl.ANY)
    vmem = pl.BlockSpec(memory_space=pltpu.VMEM)
    dma = pltpu.SemaphoreType.DMA
    b_all, c_all, lefts, dev_states, dev_offs, cum = pl.pallas_call(
        functools.partial(exchange_kernel, head_devices, seq_devices),
        out_shape=(
            jax.ShapeDtypeStruct((state_size, rows), BF16),
            jax.ShapeDtypeStruct((state_size, rows), BF16),
            jax.ShapeDtypeStruct((blocks - 1, hp, state_size), BF16),
            jax.ShapeDtypeStruct((seq_bits, hp, state_size), BF16),
            jax.ShapeDtypeStruct((seq_bits, ROWS, LANES), F32),
            jax.ShapeDtypeStruct((ROWS * blocks, BLOCK), F32),
        ),
        in_specs=[hbm, hbm, hbm, vmem],
        out_specs=(vmem,) * 6,
        scratch_shapes=[
            pltpu.VMEM(values.shape, BF16),
            pltpu.VMEM((ROWS * blocks, BLOCK), F32),
            pltpu.VMEM((blocks, hp, state_size), F32),
            pltpu.VMEM((blocks, ROWS, LANES), F32),
            pltpu.VMEM((hp, state_size), F32),
            pltpu.VMEM((seq_bits, hp, state_size), BF16),
            pltpu.VMEM((seq_bits, ROWS, LANES), F32),
            pltpu.VMEM((seq_bits, ROWS, LANES), F32),
            dma((3,)),
            dma((2, head_devices)),
            dma((2, head_devices)),
            dma((seq_bits,)),
            dma((seq_bits,)),
            dma((seq_bits,)),
            dma((seq_bits,)),
        ],
        compiler_params=pltpu.CompilerParams(
            collective_id=0, has_side_effects=True, vmem_limit_bytes=32 * 2**20
        ),
        name="gather_and_states",
    )(values, b_rows, c_rows, log_decay)

    levels = level_weight.shape[0]
    left_specs = []
    base = 0
    for r in range(local_bits):
        left_specs.append(
            pl.BlockSpec(
                (1, hp, state_size), lambda j, r=r, base=base: (base + (j >> (r + 1)), 0, 0)
            )
        )
        base += blocks >> (r + 1)
    return pl.pallas_call(
        functools.partial(output_kernel, seq_bits),
        grid=(blocks,),
        out_shape=jax.ShapeDtypeStruct(values.shape, BF16),
        in_specs=[
            pl.BlockSpec((heads, width, BLOCK), lambda j: (0, 0, j)),
            pl.BlockSpec((state_size, BLOCK), lambda j: (0, j)),
            pl.BlockSpec((state_size, BLOCK), lambda j: (0, j)),
            pl.BlockSpec((levels, heads, BLOCK), lambda j: (0, 0, j)),
            pl.BlockSpec((ROWS, BLOCK), lambda j: (j, 0)),
            *left_specs,
            pl.BlockSpec((seq_bits, hp, state_size), lambda j: (0, 0, 0)),
            pl.BlockSpec((seq_bits, ROWS, LANES), lambda j: (0, 0, 0)),
        ],
        out_specs=pl.BlockSpec((heads, width, BLOCK), lambda j: (0, 0, j)),
        scratch_shapes=[
            pltpu.VMEM((hp, BLOCK), F32),
            pltpu.VMEM((local_bits + 1, ROWS, LANES), F32),
        ],
        compiler_params=pltpu.CompilerParams(vmem_limit_bytes=32 * 2**20),
        name="outputs",
    )(values, b_all, c_all, level_weight, cum, *([lefts] * local_bits), dev_states, dev_offs)


def solution(mesh):
    return jax.shard_map(
        functools.partial(on_device, mesh.shape["head"], mesh.shape["seq"]),
        mesh=mesh,
        in_specs=(
            P("head", None, "seq"),
            P(None, ("seq", "head")),
            P(None, ("seq", "head")),
            P("head", "seq"),
            P(None, "head", "seq"),
        ),
        out_specs=P("head", None, "seq"),
        check_vma=False,
    )
```

```python
import functools

import jax
import jax.numpy as jnp
from jax import lax
from jax.experimental import pallas as pl
from jax.experimental.pallas import tpu as pltpu
from jax.sharding import PartitionSpec as P

STRETCH = 64
BLOCK = 256
STEP_BLOCKS = 4
HALF = BLOCK // 2
LANES = 128
ROWS = 8
MESH = pl.DeviceIdType.MESH
F32 = jnp.float32
BF16 = jnp.bfloat16


def flip(index, bit):
    return index + bit * (1 - 2 * lax.rem(lax.div(index, bit), 2))


def flip_all(index, mask):
    bit = 1
    while bit <= mask:
        if mask & bit:
            index = flip(index, bit)
        bit *= 2
    return index


def bits_down(count):
    bit = count // 2
    while bit:
        yield bit
        bit //= 2


def exchange_kernel(
    head_devices,
    seq_devices,
    v_hbm,
    b_hbm,
    c_hbm,
    ld_ref,
    b_all,
    c_all,
    lefts,
    dev_states,
    dev_offs,
    cum_ref,
    v_vmem,
    steps_ref,
    states,
    tots,
    group,
    send_state,
    send_tot,
    recv_tot,
    local_sem,
    gather_send,
    gather_recv,
    state_send,
    state_recv,
    tot_send,
    tot_recv,
):
    heads, width, rows = v_hbm.shape
    cols = b_hbm.shape[1]
    blocks = rows // BLOCK
    seq_bits = seq_devices.bit_length() - 1
    me = lax.axis_index("head")
    seq = lax.axis_index("seq")

    load_v = pltpu.make_async_copy(v_hbm, v_vmem, local_sem.at[0])
    load_v.start()

    partners = [("head", flip(me, bit)) for bit in bits_down(head_devices)]
    partners += [("seq", flip(seq, 2**q)) for q in range(seq_bits)]
    barrier = pltpu.get_barrier_semaphore()
    for axis, who in partners:
        pl.semaphore_signal(barrier, inc=1, device_id={axis: who}, device_id_type=MESH)
    pl.semaphore_wait(barrier, len(partners))

    def slot(full, owner):
        return full.at[:, pl.ds(pl.multiple_of(owner * cols, cols), cols)]

    pairs = ((b_hbm, b_all), (c_hbm, c_all))

    def message(a, mask):
        shard, full = pairs[a]
        bit = mask & -mask
        held = mask ^ bit
        owner = flip_all(me, held)
        return pltpu.make_async_remote_copy(
            src_ref=slot(full, owner) if held else shard,
            dst_ref=slot(full, owner),
            send_sem=gather_send.at[a, mask],
            recv_sem=gather_recv.at[a, mask],
            device_id={"head": flip(me, bit)},
            device_id_type=MESH,
        )

    def send_own(a):
        for bit in bits_down(head_devices):
            message(a, bit).start()

    def receive(a, mask):
        message(a, mask).wait_recv()
        for lower in bits_down(mask & -mask):
            message(a, mask | lower).start()

    order = [1] if head_devices > 1 else []
    for bit in bits_down(head_devices):
        order += [mask for mask in range(bit, head_devices, 2 * bit) if mask != 1]

    send_own(0)
    own = []
    for a, (shard, full) in enumerate(pairs):
        copy = pltpu.make_async_copy(shard, slot(full, me), local_sem.at[1 + a])
        copy.start()
        own.append(copy)

    steps_ref[...] = jnp.zeros_like(steps_ref)
    for j in range(blocks):
        steps_ref[pl.ds(ROWS * j, heads), :] = ld_ref[:, pl.ds(BLOCK * j, BLOCK)]
    tri = (
        lax.broadcasted_iota(jnp.int32, (BLOCK, BLOCK), 0)
        <= lax.broadcasted_iota(jnp.int32, (BLOCK, BLOCK), 1)
    ).astype(F32)
    cum_ref[...] = jnp.dot(
        steps_ref[...], tri, precision=lax.Precision.HIGHEST, preferred_element_type=F32
    )

    load_v.wait()
    own[0].wait()

    def shard_states(owner):
        per_shard = cols // BLOCK
        for k in range(per_shard):
            j = owner * per_shard + k
            cum = cum_ref[pl.ds(pl.multiple_of(ROWS * j, ROWS), ROWS), :]
            total = cum[:, BLOCK - 1 : BLOCK]
            tots[j] = jnp.broadcast_to(total, (ROWS, LANES))
            fade = jnp.exp(total - cum)
            at = pl.ds(pl.multiple_of(BLOCK * j, BLOCK), BLOCK)
            faded = [
                (v_vmem[h, :, at].astype(F32) * fade[h : h + 1, :]).astype(BF16)
                for h in range(heads)
            ]
            states[j] = lax.dot_general(
                jnp.concatenate(faded, axis=0),
                b_all[:, at],
                (((1,), (1,)), ((), ())),
                preferred_element_type=F32,
            )

    shard_states(me)
    for place, mask in enumerate(order):
        receive(0, mask)
        if place == min(1, len(order) - 1):
            send_own(1)
        shard_states(flip_all(me, mask))

    base = 0
    span = 1
    while span < blocks:
        groups = blocks // (2 * span)
        for i in range(groups):
            left = i * (2 * span) + (span - 1)
            right = left + span
            lefts[base + i] = states[left].astype(BF16)
            fade = jnp.exp(tots[right])
            for h in range(heads):
                part = pl.ds(h * width, width)
                states[right, part, :] = (
                    fade[h : h + 1, :] * states[left, part, :] + states[right, part, :]
                )
            tots[right] = tots[left] + tots[right]
        base += groups
        span *= 2

    last = blocks - 1
    my_tot = tots[last]
    off = jnp.zeros((ROWS, LANES), F32)
    group[...] = states[last]
    for q in range(seq_bits):
        partner = flip(seq, 2**q)
        right = lax.rem(lax.div(seq, 2**q), 2) == 1
        send_state[q] = group[...].astype(BF16)
        send_tot[q] = my_tot
        state_copy = pltpu.make_async_remote_copy(
            src_ref=send_state.at[q],
            dst_ref=dev_states.at[q],
            send_sem=state_send.at[q],
            recv_sem=state_recv.at[q],
            device_id={"seq": partner},
            device_id_type=MESH,
        )
        tot_copy = pltpu.make_async_remote_copy(
            src_ref=send_tot.at[q],
            dst_ref=recv_tot.at[q],
            send_sem=tot_send.at[q],
            recv_sem=tot_recv.at[q],
            device_id={"seq": partner},
            device_id_type=MESH,
        )
        tot_copy.start()
        state_copy.start()
        dev_offs[q] = off
        if q == min(1, seq_bits - 1):
            own[1].wait()
            for mask in order:
                receive(1, mask)
        tot_copy.wait()
        state_copy.wait()
        if q < seq_bits - 1:
            other = recv_tot[q]
            mine_by = jnp.where(right, 1.0, jnp.exp(other))
            other_by = jnp.where(right, jnp.exp(my_tot), 1.0)
            for h in range(heads):
                part = pl.ds(h * width, width)
                group[part, :] = mine_by[h : h + 1, :] * group[part, :] + other_by[
                    h : h + 1, :
                ] * dev_states[q, part, :].astype(F32)
            off = off + jnp.where(right, other, 0.0)
            my_tot = my_tot + other

    for a in range(2):
        for mask in range(1, head_devices):
            message(a, mask).wait_send()


def output_kernel(seq_bits, v_ref, b_ref, c_ref, w_ref, cum_ref, *rest):
    heads, width, _ = v_ref.shape
    local_bits = len(rest) - 5
    inner_bits = STEP_BLOCKS.bit_length() - 1
    left_refs = rest[:local_bits]
    dev_states, dev_offs, out_ref, acc, run = rest[local_bits:]
    j = pl.program_id(0)
    seq = lax.axis_index("seq")

    @pl.when(j == 0)
    def _():
        run[...] = jnp.zeros_like(run)

    s_at = lax.broadcasted_iota(jnp.int32, (BLOCK, BLOCK), 0)
    t_at = lax.broadcasted_iota(jnp.int32, (BLOCK, BLOCK), 1)
    causal = s_at <= t_at
    half = lax.broadcasted_iota(jnp.int32, (ROWS, BLOCK), 1) < HALF
    near = (lax.broadcasted_iota(jnp.int32, (heads, BLOCK), 1) & STRETCH) == 0
    empty = jnp.zeros((HALF, HALF), BF16)
    cums = [cum_ref[ROWS * k : ROWS * (k + 1), :] for k in range(STEP_BLOCKS)]
    totals = [cum[:, BLOCK - 1 : BLOCK] for cum in cums]
    before = [jnp.zeros((ROWS, 1), F32)]
    for total in totals:
        before.append(before[-1] + total)

    for k in range(STEP_BLOCKS):
        at = slice(k * BLOCK, (k + 1) * BLOCK)
        cum = cums[k]
        c_blk = c_ref[:, at]
        scores = lax.dot_general(
            b_ref[:, at], c_blk, (((0,), (0,)), ((), ())), preferred_element_type=F32
        )
        scores = jnp.where(causal, scores, 0.0)
        mid0 = cum[:, STRETCH - 1 : STRETCH]
        mid1 = cum[:, HALF + STRETCH - 1 : HALF + STRETCH]
        cut = cum[:, HALF - 1 : HALF]
        away = cum - jnp.where(half, mid0, mid1)
        col = jnp.exp(-away).T
        col_cut = jnp.exp(cut - cum[:, :HALF]).T
        row = jnp.exp(away)[:heads]
        w0, w1, w2 = w_ref[0, :, at], w_ref[1, :, at], w_ref[2, :, at]
        row_first = jnp.where(near, w0, w1) * row
        row_second = w0 * row
        row_cut = w2[:, HALF:] * jnp.exp(cum[:, HALF:] - cut)[:heads]

        reads = []
        for r in range(inner_bits):
            if k >> r & 1:
                state = left_refs[r][k >> (r + 1)]
                off = before[k] - before[k >> r << r]
                by = w_ref[3 + r, :, at] * jnp.exp(cum + off)[:heads]
                reads.append((jnp.dot(state, c_blk, preferred_element_type=F32), by))

        def piece(h, s0, t0, col_part, row_part):
            size = col_part.shape[0]
            factor = col_part[:, h : h + 1] * row_part[h : h + 1, :]
            return (scores[s0 : s0 + size, t0 : t0 + HALF] * factor).astype(BF16)

        for h in range(heads):
            first = jnp.concatenate(
                [
                    piece(h, 0, 0, col[:STRETCH], row_first[:, :HALF]),
                    piece(h, STRETCH, 0, col[STRETCH:HALF], row_second[:, :HALF]),
                    empty,
                ],
                axis=0,
            )
            second = jnp.concatenate(
                [
                    piece(h, 0, HALF, col_cut, row_cut),
                    piece(h, HALF, HALF, col[HALF : HALF + STRETCH], row_first[:, HALF:]),
                    piece(h, HALF + STRETCH, HALF, col[HALF + STRETCH :], row_second[:, HALF:]),
                ],
                axis=0,
            )
            mix = jnp.concatenate([first, second], axis=1)
            part = slice(h * width, (h + 1) * width)
            inner = jnp.dot(v_ref[h, :, at], mix, preferred_element_type=F32)
            for read, by in reads:
                inner += read[part, :] * by[h : h + 1, :]
            acc[part, at] = inner

    def add_level(level, state, off):
        for k in range(STEP_BLOCKS):
            at = slice(k * BLOCK, (k + 1) * BLOCK)
            read = jnp.dot(state, c_ref[:, at], preferred_element_type=F32)
            by = w_ref[level, :, at] * jnp.exp(cums[k] + (off[:, :1] + before[k]))[:heads]
            for h in range(heads):
                part = slice(h * width, (h + 1) * width)
                acc[part, at] += read[part, :] * by[h : h + 1, :]

    for r in range(inner_bits, local_bits):

        @pl.when((j >> (r - inner_bits)) & 1 == 1)
        def _(r=r):
            add_level(3 + r, left_refs[r][0], run[r])

    for q in range(seq_bits):

        @pl.when((seq >> q) & 1 == 1)
        def _(q=q):
            add_level(3 + local_bits + q, dev_states[q], run[local_bits] + dev_offs[q])

    for r in range(inner_bits, local_bits):
        fresh = (j + 1) & (2 ** (r - inner_bits) - 1) == 0
        run[r] = jnp.where(fresh, 0.0, run[r] + before[-1])
    run[local_bits] = run[local_bits] + before[-1]
    for h in range(heads):
        out_ref[h] = acc[h * width : (h + 1) * width, :].astype(BF16)


def on_device(head_devices, seq_devices, values, b_rows, c_rows, log_decay, level_weight):
    heads, width, rows = values.shape
    state_size = b_rows.shape[0]
    blocks = rows // BLOCK
    local_bits = blocks.bit_length() - 1
    seq_bits = seq_devices.bit_length() - 1
    hp = heads * width
    hbm = pl.BlockSpec(memory_space=pltpu.HBM)
    vmem = pl.BlockSpec(memory_space=pltpu.VMEM)
    dma = pltpu.SemaphoreType.DMA
    b_all, c_all, lefts, dev_states, dev_offs, cum = pl.pallas_call(
        functools.partial(exchange_kernel, head_devices, seq_devices),
        out_shape=(
            jax.ShapeDtypeStruct((state_size, rows), BF16),
            jax.ShapeDtypeStruct((state_size, rows), BF16),
            jax.ShapeDtypeStruct((blocks - 1, hp, state_size), BF16),
            jax.ShapeDtypeStruct((seq_bits, hp, state_size), BF16),
            jax.ShapeDtypeStruct((seq_bits, ROWS, LANES), F32),
            jax.ShapeDtypeStruct((ROWS * blocks, BLOCK), F32),
        ),
        in_specs=[hbm, hbm, hbm, vmem],
        out_specs=(vmem,) * 6,
        scratch_shapes=[
            pltpu.VMEM(values.shape, BF16),
            pltpu.VMEM((ROWS * blocks, BLOCK), F32),
            pltpu.VMEM((blocks, hp, state_size), F32),
            pltpu.VMEM((blocks, ROWS, LANES), F32),
            pltpu.VMEM((hp, state_size), F32),
            pltpu.VMEM((seq_bits, hp, state_size), BF16),
            pltpu.VMEM((seq_bits, ROWS, LANES), F32),
            pltpu.VMEM((seq_bits, ROWS, LANES), F32),
            dma((3,)),
            dma((2, head_devices)),
            dma((2, head_devices)),
            dma((seq_bits,)),
            dma((seq_bits,)),
            dma((seq_bits,)),
            dma((seq_bits,)),
        ],
        compiler_params=pltpu.CompilerParams(
            collective_id=0, has_side_effects=True, vmem_limit_bytes=60 * 2**20
        ),
        name="gather_and_states",
    )(values, b_rows, c_rows, log_decay)

    levels = level_weight.shape[0]
    step = STEP_BLOCKS * BLOCK
    inner_bits = STEP_BLOCKS.bit_length() - 1
    left_specs = []
    base = 0
    for r in range(local_bits):
        if r < inner_bits:
            per_step = STEP_BLOCKS >> (r + 1)
            spec = pl.BlockSpec(
                (per_step, hp, state_size), lambda j, at=base // per_step: (at + j, 0, 0)
            )
        else:
            spec = pl.BlockSpec(
                (1, hp, state_size),
                lambda j, at=base, shift=r + 1 - inner_bits: (at + (j >> shift), 0, 0),
            )
        left_specs.append(spec)
        base += blocks >> (r + 1)
    return pl.pallas_call(
        functools.partial(output_kernel, seq_bits),
        grid=(blocks // STEP_BLOCKS,),
        out_shape=jax.ShapeDtypeStruct(values.shape, BF16),
        in_specs=[
            pl.BlockSpec((heads, width, step), lambda j: (0, 0, j)),
            pl.BlockSpec((state_size, step), lambda j: (0, j)),
            pl.BlockSpec((state_size, step), lambda j: (0, j)),
            pl.BlockSpec((levels, heads, step), lambda j: (0, 0, j)),
            pl.BlockSpec((ROWS * STEP_BLOCKS, BLOCK), lambda j: (j, 0)),
            *left_specs,
            pl.BlockSpec((seq_bits, hp, state_size), lambda j: (0, 0, 0)),
            pl.BlockSpec((seq_bits, ROWS, LANES), lambda j: (0, 0, 0)),
        ],
        out_specs=pl.BlockSpec((heads, width, step), lambda j: (0, 0, j)),
        scratch_shapes=[
            pltpu.VMEM((hp, step), F32),
            pltpu.VMEM((local_bits + 1, ROWS, LANES), F32),
        ],
        compiler_params=pltpu.CompilerParams(vmem_limit_bytes=60 * 2**20),
        name="outputs",
    )(values, b_all, c_all, level_weight, cum, *([lefts] * local_bits), dev_states, dev_offs)


def solution(mesh):
    return jax.shard_map(
        functools.partial(on_device, mesh.shape["head"], mesh.shape["seq"]),
        mesh=mesh,
        in_specs=(
            P("head", None, "seq"),
            P(None, ("seq", "head")),
            P(None, ("seq", "head")),
            P("head", "seq"),
            P(None, "head", "seq"),
        ),
        out_specs=P("head", None, "seq"),
        check_vma=False,
    )
```

```python
import functools

import jax
import jax.numpy as jnp
from jax import lax
from jax.experimental import pallas as pl
from jax.experimental.pallas import tpu as pltpu
from jax.sharding import PartitionSpec as P

STRETCH = 64
BLOCK = 256
STEP_BLOCKS = 4
HALF = BLOCK // 2
LANES = 128
ROWS = 8
MESH = pl.DeviceIdType.MESH
F32 = jnp.float32
BF16 = jnp.bfloat16


def flip(index, bit):
    return index + bit * (1 - 2 * lax.rem(lax.div(index, bit), 2))


def flip_all(index, mask):
    bit = 1
    while bit <= mask:
        if mask & bit:
            index = flip(index, bit)
        bit *= 2
    return index


def bits_down(count):
    bit = count // 2
    while bit:
        yield bit
        bit //= 2


def scan_kernel(
    head_devices,
    seq_devices,
    v_hbm,
    b_hbm,
    c_hbm,
    ld_hbm,
    w_hbm,
    out_hbm,
    v_ref,
    b_all,
    c_all,
    ld_ref,
    w_ref,
    out_ref,
    acc,
    cum_ref,
    steps_ref,
    states,
    lefts,
    tots,
    befores,
    group,
    dev_states,
    dev_offs,
    send_state,
    send_tot,
    recv_tot,
    local_sem,
    out_sem,
    gather_send,
    gather_recv,
    state_send,
    state_recv,
    tot_send,
    tot_recv,
):
    heads, width, rows = v_hbm.shape
    cols = b_hbm.shape[1]
    blocks = rows // BLOCK
    seq_bits = seq_devices.bit_length() - 1
    me = lax.axis_index("head")
    seq = lax.axis_index("seq")

    load_ld = pltpu.make_async_copy(ld_hbm, ld_ref, local_sem.at[3])
    load_ld.start()
    load_v = pltpu.make_async_copy(v_hbm, v_ref, local_sem.at[0])
    load_v.start()

    partners = [("head", flip(me, bit)) for bit in bits_down(head_devices)]
    partners += [("seq", flip(seq, 2**q)) for q in range(seq_bits)]
    barrier = pltpu.get_barrier_semaphore()
    for axis, who in partners:
        pl.semaphore_signal(barrier, inc=1, device_id={axis: who}, device_id_type=MESH)
    pl.semaphore_wait(barrier, len(partners))

    def slot(full, owner):
        return full.at[:, pl.ds(pl.multiple_of(owner * cols, cols), cols)]

    pairs = ((b_hbm, b_all), (c_hbm, c_all))

    def message(a, mask):
        shard, full = pairs[a]
        bit = mask & -mask
        held = mask ^ bit
        owner = flip_all(me, held)
        return pltpu.make_async_remote_copy(
            src_ref=slot(full, owner) if held else shard,
            dst_ref=slot(full, owner),
            send_sem=gather_send.at[a, mask],
            recv_sem=gather_recv.at[a, mask],
            device_id={"head": flip(me, bit)},
            device_id_type=MESH,
        )

    def send_own(a):
        for bit in bits_down(head_devices):
            message(a, bit).start()

    def receive(a, mask):
        message(a, mask).wait_recv()
        for lower in bits_down(mask & -mask):
            message(a, mask | lower).start()

    order = [1] if head_devices > 1 else []
    for bit in bits_down(head_devices):
        order += [mask for mask in range(bit, head_devices, 2 * bit) if mask != 1]

    send_own(0)
    own = []
    for a, (shard, full) in enumerate(pairs):
        copy = pltpu.make_async_copy(shard, slot(full, me), local_sem.at[1 + a])
        copy.start()
        own.append(copy)
    load_w = pltpu.make_async_copy(w_hbm, w_ref, local_sem.at[4])
    load_w.start()

    steps_ref[...] = jnp.zeros_like(steps_ref)
    load_ld.wait()
    for j in range(blocks):
        steps_ref[pl.ds(ROWS * j, heads), :] = ld_ref[:, pl.ds(BLOCK * j, BLOCK)]
    tri = (
        lax.broadcasted_iota(jnp.int32, (BLOCK, BLOCK), 0)
        <= lax.broadcasted_iota(jnp.int32, (BLOCK, BLOCK), 1)
    ).astype(F32)
    cum_ref[...] = jnp.dot(
        steps_ref[...], tri, precision=lax.Precision.HIGHEST, preferred_element_type=F32
    )

    load_v.wait()
    own[0].wait()

    def shard_states(owner):
        per_shard = cols // BLOCK
        for k in range(per_shard):
            j = owner * per_shard + k
            cum = cum_ref[pl.ds(pl.multiple_of(ROWS * j, ROWS), ROWS), :]
            total = cum[:, BLOCK - 1 : BLOCK]
            tots[j] = jnp.broadcast_to(total, (ROWS, LANES))
            fade = jnp.exp(total - cum)
            at = pl.ds(pl.multiple_of(BLOCK * j, BLOCK), BLOCK)
            faded = [
                (v_ref[h, :, at].astype(F32) * fade[h : h + 1, :]).astype(BF16)
                for h in range(heads)
            ]
            states[j] = lax.dot_general(
                jnp.concatenate(faded, axis=0),
                b_all[:, at],
                (((1,), (1,)), ((), ())),
                preferred_element_type=F32,
            )

    shard_states(me)
    for place, mask in enumerate(order):
        receive(0, mask)
        if place == min(1, len(order) - 1):
            send_own(1)
        shard_states(flip_all(me, mask))

    before = jnp.zeros((ROWS, LANES), F32)
    for j in range(blocks):
        befores[j] = before
        before = before + tots[j]

    base = 0
    span = 1
    while span < blocks:
        groups = blocks // (2 * span)
        for i in range(groups):
            left = i * (2 * span) + (span - 1)
            right = left + span
            lefts[base + i] = states[left].astype(BF16)
            fade = jnp.exp(tots[right])
            for h in range(heads):
                part = pl.ds(h * width, width)
                states[right, part, :] = (
                    fade[h : h + 1, :] * states[left, part, :] + states[right, part, :]
                )
            tots[right] = tots[left] + tots[right]
        base += groups
        span *= 2

    last = blocks - 1
    group[...] = states[last]
    send_tot[0] = tots[last]
    dev_offs[0] = jnp.zeros((ROWS, LANES), F32)

    def swaps(q):
        partner = flip(seq, 2**q)
        return [
            pltpu.make_async_remote_copy(
                src_ref=src.at[q],
                dst_ref=dst.at[q],
                send_sem=send_sem.at[q],
                recv_sem=recv_sem.at[q],
                device_id={"seq": partner},
                device_id_type=MESH,
            )
            for src, dst, send_sem, recv_sem in (
                (send_tot, recv_tot, tot_send, tot_recv),
                (send_state, dev_states, state_send, state_recv),
            )
        ]

    def begin(q):
        send_state[q] = group[...].astype(BF16)
        for copy in swaps(q):
            copy.start()

    def finish(q):
        for copy in swaps(q):
            copy.wait()
        if q < seq_bits - 1:
            right = lax.rem(lax.div(seq, 2**q), 2) == 1
            mine, other = send_tot[q], recv_tot[q]
            mine_by = jnp.where(right, 1.0, jnp.exp(other))
            other_by = jnp.where(right, jnp.exp(mine), 1.0)
            for h in range(heads):
                part = pl.ds(h * width, width)
                group[part, :] = mine_by[h : h + 1, :] * group[part, :] + other_by[
                    h : h + 1, :
                ] * dev_states[q, part, :].astype(F32)
            dev_offs[q + 1] = dev_offs[q] + jnp.where(right, other, 0.0)
            send_tot[q + 1] = mine + other
            begin(q + 1)

    begin(0)
    own[1].wait()
    for mask in order:
        receive(1, mask)
    load_w.wait()
    finish(0)

    local_bits = blocks.bit_length() - 1
    inner_bits = STEP_BLOCKS.bit_length() - 1
    steps = blocks // STEP_BLOCKS
    left_base = [blocks - (blocks >> r) for r in range(local_bits)]
    s_at = lax.broadcasted_iota(jnp.int32, (BLOCK, BLOCK), 0)
    t_at = lax.broadcasted_iota(jnp.int32, (BLOCK, BLOCK), 1)
    causal = s_at <= t_at
    near_at = lax.broadcasted_iota(jnp.int32, (heads, BLOCK), 1)
    near = (near_at < STRETCH) | ((near_at >= HALF) & (near_at < HALF + STRETCH))
    empty = jnp.zeros((HALF, HALF), BF16)

    def tokens(j):
        return pl.ds(pl.multiple_of(j * BLOCK, BLOCK), BLOCK)

    def cum_of(j):
        return cum_ref[pl.ds(pl.multiple_of(ROWS * j, ROWS), ROWS), :]

    def level_scale(level, j, off):
        return w_ref[level, :, tokens(j)] * jnp.exp(cum_of(j) + off[:, :1])[:heads]

    def near_levels(step, k):
        j = step * STEP_BLOCKS + k
        at = tokens(j)
        cum = cum_of(j)
        c_blk = c_all[:, at]
        scores = lax.dot_general(
            b_all[:, at], c_blk, (((0,), (0,)), ((), ())), preferred_element_type=F32
        )
        scores = jnp.where(causal, scores, 0.0)
        cut = cum[:, HALF - 1 : HALF]
        col = jnp.exp(cut - cum).T
        row = jnp.exp(cum - cut)[:heads]
        w0, w1, w2 = w_ref[0, :, at], w_ref[1, :, at], w_ref[2, :, at]
        row_first = jnp.where(near, w0, w1) * row
        row_second = w0 * row
        row_cut = w2[:, HALF:] * row[:, HALF:]

        reads = []
        for r in range(inner_bits):
            if k >> r & 1:
                per_step = STEP_BLOCKS >> (r + 1)
                state = lefts[left_base[r] + step * per_step + (k >> (r + 1))]
                off = befores[j] - befores[step * STEP_BLOCKS + (k >> r << r)]
                by = level_scale(3 + r, j, off)
                reads.append((jnp.dot(state, c_blk, preferred_element_type=F32), by))

        def piece(h, s0, t0, size, row_part):
            factor = col[s0 : s0 + size, h : h + 1] * row_part[h : h + 1, :]
            return (scores[s0 : s0 + size, t0 : t0 + HALF] * factor).astype(BF16)

        for h in range(heads):
            first = [
                piece(h, 0, 0, STRETCH, row_first[:, :HALF]),
                piece(h, STRETCH, 0, STRETCH, row_second[:, :HALF]),
                empty,
            ]
            second = [
                piece(h, 0, HALF, HALF, row_cut),
                piece(h, HALF, HALF, STRETCH, row_first[:, HALF:]),
                piece(h, HALF + STRETCH, HALF, STRETCH, row_second[:, HALF:]),
            ]
            mix = jnp.concatenate(
                [jnp.concatenate(first, axis=0), jnp.concatenate(second, axis=0)], axis=1
            )
            part = slice(h * width, (h + 1) * width)
            inner = jnp.dot(v_ref[h, :, at], mix, preferred_element_type=F32)
            for read, by in reads:
                inner += read[part, :] * by[h : h + 1, :]
            acc[part, at] = inner

    def add_level(level, step, state, off_of):
        for k in range(STEP_BLOCKS):
            j = step * STEP_BLOCKS + k
            at = tokens(j)
            read = jnp.dot(state, c_all[:, at], preferred_element_type=F32)
            by = level_scale(level, j, off_of(j))
            for h in range(heads):
                part = slice(h * width, (h + 1) * width)
                acc[part, at] += read[part, :] * by[h : h + 1, :]

    def local_step(step, carry):
        for k in range(STEP_BLOCKS):
            near_levels(step, k)
        for r in range(inner_bits, local_bits):
            apart = 2 ** (r - inner_bits)

            @pl.when(lax.rem(lax.div(step, apart), 2) == 1)
            def _(r=r, apart=apart):
                state = lefts[left_base[r] + lax.div(step, 2 * apart)]
                start = lax.div(step, apart) * (apart * STEP_BLOCKS)
                add_level(3 + r, step, state, lambda j: befores[j] - befores[start])

        for q in range(1, min(seq_bits, steps + 1)):
            pl.when(step == q - 1)(functools.partial(finish, q))
        return carry

    lax.fori_loop(0, steps, local_step, 0)
    for q in range(steps + 1, seq_bits):
        finish(q)

    def store(step):
        at = pl.ds(pl.multiple_of(step * (STEP_BLOCKS * BLOCK), BLOCK), STEP_BLOCKS * BLOCK)
        return pltpu.make_async_copy(
            out_ref.at[:, :, at], out_hbm.at[:, :, at], out_sem.at[step]
        )

    def last_step(step, carry):
        for q in range(seq_bits):

            @pl.when(lax.rem(lax.div(seq, 2**q), 2) == 1)
            def _(q=q):
                add_level(
                    3 + local_bits + q, step, dev_states[q], lambda j: befores[j] + dev_offs[q]
                )

        at = pl.ds(pl.multiple_of(step * (STEP_BLOCKS * BLOCK), BLOCK), STEP_BLOCKS * BLOCK)
        for h in range(heads):
            out_ref[h, :, at] = acc[h * width : (h + 1) * width, at].astype(BF16)
        store(step).start()
        return carry

    lax.fori_loop(0, steps, last_step, 0)

    for a in range(2):
        for mask in range(1, head_devices):
            message(a, mask).wait_send()
    for step in range(steps):
        store(step).wait()


def on_device(head_devices, seq_devices, values, b_rows, c_rows, log_decay, level_weight):
    heads, width, rows = values.shape
    state_size = b_rows.shape[0]
    blocks = rows // BLOCK
    seq_bits = seq_devices.bit_length() - 1
    hp = heads * width
    hbm = pl.BlockSpec(memory_space=pltpu.HBM)
    dma = pltpu.SemaphoreType.DMA
    return pl.pallas_call(
        functools.partial(scan_kernel, head_devices, seq_devices),
        out_shape=jax.ShapeDtypeStruct(values.shape, BF16),
        in_specs=[hbm] * 5,
        out_specs=hbm,
        scratch_shapes=[
            pltpu.VMEM(values.shape, BF16),
            pltpu.VMEM((state_size, rows), BF16),
            pltpu.VMEM((state_size, rows), BF16),
            pltpu.VMEM(log_decay.shape, F32),
            pltpu.VMEM(level_weight.shape, F32),
            pltpu.VMEM(values.shape, BF16),
            pltpu.VMEM((hp, rows), F32),
            pltpu.VMEM((ROWS * blocks, BLOCK), F32),
            pltpu.VMEM((ROWS * blocks, BLOCK), F32),
            pltpu.VMEM((blocks, hp, state_size), F32),
            pltpu.VMEM((blocks - 1, hp, state_size), BF16),
            pltpu.VMEM((blocks, ROWS, LANES), F32),
            pltpu.VMEM((blocks, ROWS, LANES), F32),
            pltpu.VMEM((hp, state_size), F32),
            pltpu.VMEM((seq_bits, hp, state_size), BF16),
            pltpu.VMEM((seq_bits, ROWS, LANES), F32),
            pltpu.VMEM((seq_bits, hp, state_size), BF16),
            pltpu.VMEM((seq_bits, ROWS, LANES), F32),
            pltpu.VMEM((seq_bits, ROWS, LANES), F32),
            dma((5,)),
            dma((blocks // STEP_BLOCKS,)),
            dma((2, head_devices)),
            dma((2, head_devices)),
            dma((seq_bits,)),
            dma((seq_bits,)),
            dma((seq_bits,)),
            dma((seq_bits,)),
        ],
        compiler_params=pltpu.CompilerParams(
            collective_id=0, has_side_effects=True, vmem_limit_bytes=60 * 2**20
        ),
        name="scan",
    )(values, b_rows, c_rows, log_decay, level_weight)


def solution(mesh):
    return jax.shard_map(
        functools.partial(on_device, mesh.shape["head"], mesh.shape["seq"]),
        mesh=mesh,
        in_specs=(
            P("head", None, "seq"),
            P(None, ("seq", "head")),
            P(None, ("seq", "head")),
            P("head", "seq"),
            P(None, "head", "seq"),
        ),
        out_specs=P("head", None, "seq"),
        check_vma=False,
    )
```

```python
import functools

import jax
import jax.numpy as jnp
from jax import lax
from jax.experimental import pallas as pl
from jax.experimental.pallas import tpu as pltpu
from jax.sharding import PartitionSpec as P

STRETCH = 64
BLOCK = 256
STEP_BLOCKS = 4
HALF = BLOCK // 2
LANES = 128
ROWS = 8
MESH = pl.DeviceIdType.MESH
F32 = jnp.float32
BF16 = jnp.bfloat16


def flip(index, bit):
    return index + bit * (1 - 2 * lax.rem(lax.div(index, bit), 2))


def flip_all(index, mask):
    bit = 1
    while bit <= mask:
        if mask & bit:
            index = flip(index, bit)
        bit *= 2
    return index


def bits_down(count):
    bit = count // 2
    while bit:
        yield bit
        bit //= 2


def scan_kernel(
    head_devices,
    seq_devices,
    v_hbm,
    b_hbm,
    c_hbm,
    ld_hbm,
    w_hbm,
    out_hbm,
    v_ref,
    b_all,
    c_all,
    ld_ref,
    w_ref,
    out_ref,
    acc,
    cum_ref,
    steps_ref,
    states,
    lefts,
    tots,
    befores,
    group,
    dev_states,
    dev_offs,
    send_state,
    send_tot,
    recv_tot,
    local_sem,
    out_sem,
    gather_send,
    gather_recv,
    state_send,
    state_recv,
    tot_send,
    tot_recv,
):
    heads, width, rows = v_hbm.shape
    cols = b_hbm.shape[1]
    blocks = rows // BLOCK
    seq_bits = seq_devices.bit_length() - 1
    me = lax.axis_index("head")
    seq = lax.axis_index("seq")

    load_ld = pltpu.make_async_copy(ld_hbm, ld_ref, local_sem.at[3])
    load_ld.start()
    load_v = pltpu.make_async_copy(v_hbm, v_ref, local_sem.at[0])
    load_v.start()

    partners = [("head", flip(me, bit)) for bit in bits_down(head_devices)]
    partners += [("seq", flip(seq, 2**q)) for q in range(seq_bits)]
    barrier = pltpu.get_barrier_semaphore()
    for axis, who in partners:
        pl.semaphore_signal(barrier, inc=1, device_id={axis: who}, device_id_type=MESH)
    pl.semaphore_wait(barrier, len(partners))

    def slot(full, owner):
        return full.at[:, pl.ds(pl.multiple_of(owner * cols, cols), cols)]

    pairs = ((b_hbm, b_all), (c_hbm, c_all))

    def message(a, mask):
        shard, full = pairs[a]
        bit = mask & -mask
        held = mask ^ bit
        owner = flip_all(me, held)
        return pltpu.make_async_remote_copy(
            src_ref=slot(full, owner) if held else shard,
            dst_ref=slot(full, owner),
            send_sem=gather_send.at[a, mask],
            recv_sem=gather_recv.at[a, mask],
            device_id={"head": flip(me, bit)},
            device_id_type=MESH,
        )

    def send_own(a, least=1):
        for bit in bits_down(head_devices):
            if bit >= least:
                message(a, bit).start()

    def receive(a, mask):
        message(a, mask).wait_recv()
        for lower in bits_down(mask & -mask):
            message(a, mask | lower).start()

    order = [1] if head_devices > 1 else []
    for bit in bits_down(head_devices):
        order += [mask for mask in range(bit, head_devices, 2 * bit) if mask != 1]

    send_own(0)
    if head_devices > 1:
        message(1, 1).start()
    own = []
    for a, (shard, full) in enumerate(pairs):
        copy = pltpu.make_async_copy(shard, slot(full, me), local_sem.at[1 + a])
        copy.start()
        own.append(copy)
    load_w = pltpu.make_async_copy(w_hbm, w_ref, local_sem.at[4])
    load_w.start()

    steps_ref[...] = jnp.zeros_like(steps_ref)
    load_ld.wait()
    for j in range(blocks):
        steps_ref[pl.ds(ROWS * j, heads), :] = ld_ref[:, pl.ds(BLOCK * j, BLOCK)]
    tri = (
        lax.broadcasted_iota(jnp.int32, (BLOCK, BLOCK), 0)
        <= lax.broadcasted_iota(jnp.int32, (BLOCK, BLOCK), 1)
    ).astype(F32)
    cum_ref[...] = jnp.dot(
        steps_ref[...], tri, precision=lax.Precision.HIGHEST, preferred_element_type=F32
    )

    def shard_states(owner):
        per_shard = cols // BLOCK
        for k in range(per_shard):
            j = owner * per_shard + k
            cum = cum_ref[pl.ds(pl.multiple_of(ROWS * j, ROWS), ROWS), :]
            total = cum[:, BLOCK - 1 : BLOCK]
            tots[j] = jnp.broadcast_to(total, (ROWS, LANES))
            fade = jnp.exp(total - cum)
            at = pl.ds(pl.multiple_of(BLOCK * j, BLOCK), BLOCK)
            faded = [
                (v_ref[h, :, at].astype(F32) * fade[h : h + 1, :]).astype(BF16)
                for h in range(heads)
            ]
            states[j] = lax.dot_general(
                jnp.concatenate(faded, axis=0),
                b_all[:, at],
                (((1,), (1,)), ((), ())),
                preferred_element_type=F32,
            )

    inner_bits = STEP_BLOCKS.bit_length() - 1
    step_shards = max(1, STEP_BLOCKS * BLOCK // cols)
    steps = blocks // STEP_BLOCKS

    def merge(base, span, first, count):
        for i in range(count):
            left = (first + i) * (2 * span) + (span - 1)
            right = left + span
            lefts[base + first + i] = states[left].astype(BF16)
            fade = jnp.exp(tots[right])
            for h in range(heads):
                part = pl.ds(h * width, width)
                states[right, part, :] = (
                    fade[h : h + 1, :] * states[left, part, :] + states[right, part, :]
                )
            tots[right] = tots[left] + tots[right]

    def merge_step(step):
        for r in range(inner_bits):
            per_step = STEP_BLOCKS >> (r + 1)
            merge(blocks - (blocks >> r), 2**r, step * per_step, per_step)

    own_step = lax.div(me, step_shards)

    def step_at(i):
        where = own_step
        for bit in bits_down(steps):
            set_here = lax.rem(lax.div(i, bit), 2)
            where = where + set_here * bit * (1 - 2 * lax.rem(lax.div(where, bit), 2))
        return where

    load_v.wait()
    own[0].wait()
    shard_states(me)
    for mask in order:
        if mask < step_shards:
            receive(0, mask)
            shard_states(flip_all(me, mask))
    merge_step(own_step)

    def other_states():
        later = [mask for mask in order if mask >= step_shards]
        sent = False
        for mask in later:
            receive(0, mask)
            if mask != 1 and not sent:
                send_own(1, 2)
                sent = True
            shard_states(flip_all(me, mask))
        if not sent:
            send_own(1, 2)
        for i in range(1, steps):
            merge_step(step_at(i))
        before = jnp.zeros((ROWS, LANES), F32)
        for j in range(blocks):
            cum = cum_ref[ROWS * j : ROWS * (j + 1), :]
            befores[j] = before
            before = before + jnp.broadcast_to(cum[:, BLOCK - 1 : BLOCK], (ROWS, LANES))
        for r in range(inner_bits, blocks.bit_length() - 1):
            merge(blocks - (blocks >> r), 2**r, 0, blocks >> (r + 1))
        last = blocks - 1
        group[...] = states[last]
        send_tot[0] = tots[last]
        dev_offs[0] = jnp.zeros((ROWS, LANES), F32)
        begin(0)

    def swaps(q):
        partner = flip(seq, 2**q)
        return [
            pltpu.make_async_remote_copy(
                src_ref=src.at[q],
                dst_ref=dst.at[q],
                send_sem=send_sem.at[q],
                recv_sem=recv_sem.at[q],
                device_id={"seq": partner},
                device_id_type=MESH,
            )
            for src, dst, send_sem, recv_sem in (
                (send_tot, recv_tot, tot_send, tot_recv),
                (send_state, dev_states, state_send, state_recv),
            )
        ]

    def begin(q):
        send_state[q] = group[...].astype(BF16)
        for copy in swaps(q):
            copy.start()

    def finish(q):
        for copy in swaps(q):
            copy.wait()
        if q < seq_bits - 1:
            right = lax.rem(lax.div(seq, 2**q), 2) == 1
            mine, other = send_tot[q], recv_tot[q]
            mine_by = jnp.where(right, 1.0, jnp.exp(other))
            other_by = jnp.where(right, jnp.exp(mine), 1.0)
            for h in range(heads):
                part = pl.ds(h * width, width)
                group[part, :] = mine_by[h : h + 1, :] * group[part, :] + other_by[
                    h : h + 1, :
                ] * dev_states[q, part, :].astype(F32)
            dev_offs[q + 1] = dev_offs[q] + jnp.where(right, other, 0.0)
            send_tot[q + 1] = mine + other
            begin(q + 1)

    own[1].wait()
    for mask in order:
        if mask < step_shards:
            receive(1, mask)
    load_w.wait()

    local_bits = blocks.bit_length() - 1
    left_base = [blocks - (blocks >> r) for r in range(local_bits)]
    s_at = lax.broadcasted_iota(jnp.int32, (BLOCK, BLOCK), 0)
    t_at = lax.broadcasted_iota(jnp.int32, (BLOCK, BLOCK), 1)
    causal = s_at <= t_at
    near_at = lax.broadcasted_iota(jnp.int32, (heads, BLOCK), 1)
    near = (near_at < STRETCH) | ((near_at >= HALF) & (near_at < HALF + STRETCH))
    empty = jnp.zeros((HALF, HALF), BF16)

    def tokens(j):
        return pl.ds(pl.multiple_of(j * BLOCK, BLOCK), BLOCK)

    def cum_of(j):
        return cum_ref[pl.ds(pl.multiple_of(ROWS * j, ROWS), ROWS), :]

    def level_scale(level, j, off):
        return w_ref[level, :, tokens(j)] * jnp.exp(cum_of(j) + off[:, :1])[:heads]

    def near_levels(step, k):
        j = step * STEP_BLOCKS + k
        at = tokens(j)
        cum = cum_of(j)
        c_blk = c_all[:, at]
        scores = lax.dot_general(
            b_all[:, at], c_blk, (((0,), (0,)), ((), ())), preferred_element_type=F32
        )
        scores = jnp.where(causal, scores, 0.0)
        cut = cum[:, HALF - 1 : HALF]
        col = jnp.exp(cut - cum).T
        row = jnp.exp(cum - cut)[:heads]
        w0, w1, w2 = w_ref[0, :, at], w_ref[1, :, at], w_ref[2, :, at]
        row_first = jnp.where(near, w0, w1) * row
        row_second = w0 * row
        row_cut = w2[:, HALF:] * row[:, HALF:]

        reads = []
        for r in range(inner_bits):
            if k >> r & 1:
                per_step = STEP_BLOCKS >> (r + 1)
                state = lefts[left_base[r] + step * per_step + (k >> (r + 1))]
                off = jnp.zeros((ROWS, 1), F32)
                for i in range(k >> r << r, k):
                    off = off + cum_of(step * STEP_BLOCKS + i)[:, BLOCK - 1 : BLOCK]
                by = level_scale(3 + r, j, off)
                reads.append((jnp.dot(state, c_blk, preferred_element_type=F32), by))

        def piece(h, s0, t0, size, row_part):
            factor = col[s0 : s0 + size, h : h + 1] * row_part[h : h + 1, :]
            return (scores[s0 : s0 + size, t0 : t0 + HALF] * factor).astype(BF16)

        for h in range(heads):
            first = [
                piece(h, 0, 0, STRETCH, row_first[:, :HALF]),
                piece(h, STRETCH, 0, STRETCH, row_second[:, :HALF]),
                empty,
            ]
            second = [
                piece(h, 0, HALF, HALF, row_cut),
                piece(h, HALF, HALF, STRETCH, row_first[:, HALF:]),
                piece(h, HALF + STRETCH, HALF, STRETCH, row_second[:, HALF:]),
            ]
            mix = jnp.concatenate(
                [jnp.concatenate(first, axis=0), jnp.concatenate(second, axis=0)], axis=1
            )
            part = slice(h * width, (h + 1) * width)
            inner = jnp.dot(v_ref[h, :, at], mix, preferred_element_type=F32)
            for read, by in reads:
                inner += read[part, :] * by[h : h + 1, :]
            acc[part, at] = inner

    def add_level(level, step, state, off_of):
        for k in range(STEP_BLOCKS):
            j = step * STEP_BLOCKS + k
            at = tokens(j)
            read = jnp.dot(state, c_all[:, at], preferred_element_type=F32)
            by = level_scale(level, j, off_of(j))
            for h in range(heads):
                part = slice(h * width, (h + 1) * width)
                acc[part, at] += read[part, :] * by[h : h + 1, :]

    shards_of = [
        [mask for mask in order if mask >= step_shards and mask // step_shards == i]
        for i in range(steps)
    ]

    def near_step(i, carry):
        for at in range(1, steps):

            @pl.when(i == at)
            def _(at=at):
                for mask in shards_of[at]:
                    receive(1, mask)

        step = step_at(i)
        for k in range(STEP_BLOCKS):
            near_levels(step, k)
        pl.when(i == 0)(other_states)
        for q in range(min(seq_bits - 1, steps - 2)):
            pl.when(i == q + 1)(functools.partial(finish, q))
        return carry

    lax.fori_loop(0, steps, near_step, 0)
    for q in range(min(seq_bits - 1, steps - 2), seq_bits - 1):
        finish(q)

    def far_step(step, carry):
        for r in range(inner_bits, local_bits):
            apart = 2 ** (r - inner_bits)

            @pl.when(lax.rem(lax.div(step, apart), 2) == 1)
            def _(r=r, apart=apart):
                state = lefts[left_base[r] + lax.div(step, 2 * apart)]
                start = lax.div(step, apart) * (apart * STEP_BLOCKS)
                add_level(3 + r, step, state, lambda j: befores[j] - befores[start])

        return carry

    lax.fori_loop(0, steps, far_step, 0)
    finish(seq_bits - 1)

    def store(step):
        at = pl.ds(pl.multiple_of(step * (STEP_BLOCKS * BLOCK), BLOCK), STEP_BLOCKS * BLOCK)
        return pltpu.make_async_copy(
            out_ref.at[:, :, at], out_hbm.at[:, :, at], out_sem.at[step]
        )

    def last_step(step, carry):
        for k in range(STEP_BLOCKS):
            j = step * STEP_BLOCKS + k
            at = tokens(j)
            reads = []
            for q in range(seq_bits):
                has = lax.rem(lax.div(seq, 2**q), 2) == 1
                by = level_scale(3 + local_bits + q, j, befores[j] + dev_offs[q])
                read = jnp.dot(dev_states[q], c_all[:, at], preferred_element_type=F32)
                reads.append((read, jnp.where(has, by, 0.0)))
            for h in range(heads):
                part = slice(h * width, (h + 1) * width)
                total = acc[part, at]
                for read, by in reads:
                    total += read[part, :] * by[h : h + 1, :]
                out_ref[h, :, at] = total.astype(BF16)
        store(step).start()
        return carry

    lax.fori_loop(0, steps, last_step, 0)

    for a in range(2):
        for mask in range(1, head_devices):
            message(a, mask).wait_send()
    for step in range(steps):
        store(step).wait()


def on_device(head_devices, seq_devices, values, b_rows, c_rows, log_decay, level_weight):
    heads, width, rows = values.shape
    state_size = b_rows.shape[0]
    blocks = rows // BLOCK
    seq_bits = seq_devices.bit_length() - 1
    hp = heads * width
    hbm = pl.BlockSpec(memory_space=pltpu.HBM)
    dma = pltpu.SemaphoreType.DMA
    return pl.pallas_call(
        functools.partial(scan_kernel, head_devices, seq_devices),
        out_shape=jax.ShapeDtypeStruct(values.shape, BF16),
        in_specs=[hbm] * 5,
        out_specs=hbm,
        scratch_shapes=[
            pltpu.VMEM(values.shape, BF16),
            pltpu.VMEM((state_size, rows), BF16),
            pltpu.VMEM((state_size, rows), BF16),
            pltpu.VMEM(log_decay.shape, F32),
            pltpu.VMEM(level_weight.shape, F32),
            pltpu.VMEM(values.shape, BF16),
            pltpu.VMEM((hp, rows), F32),
            pltpu.VMEM((ROWS * blocks, BLOCK), F32),
            pltpu.VMEM((ROWS * blocks, BLOCK), F32),
            pltpu.VMEM((blocks, hp, state_size), F32),
            pltpu.VMEM((blocks - 1, hp, state_size), BF16),
            pltpu.VMEM((blocks, ROWS, LANES), F32),
            pltpu.VMEM((blocks, ROWS, LANES), F32),
            pltpu.VMEM((hp, state_size), F32),
            pltpu.VMEM((seq_bits, hp, state_size), BF16),
            pltpu.VMEM((seq_bits, ROWS, LANES), F32),
            pltpu.VMEM((seq_bits, hp, state_size), BF16),
            pltpu.VMEM((seq_bits, ROWS, LANES), F32),
            pltpu.VMEM((seq_bits, ROWS, LANES), F32),
            dma((5,)),
            dma((blocks // STEP_BLOCKS,)),
            dma((2, head_devices)),
            dma((2, head_devices)),
            dma((seq_bits,)),
            dma((seq_bits,)),
            dma((seq_bits,)),
            dma((seq_bits,)),
        ],
        compiler_params=pltpu.CompilerParams(
            collective_id=0, has_side_effects=True, vmem_limit_bytes=60 * 2**20
        ),
        name="scan",
    )(values, b_rows, c_rows, log_decay, level_weight)


def solution(mesh):
    return jax.shard_map(
        functools.partial(on_device, mesh.shape["head"], mesh.shape["seq"]),
        mesh=mesh,
        in_specs=(
            P("head", None, "seq"),
            P(None, ("seq", "head")),
            P(None, ("seq", "head")),
            P("head", "seq"),
            P(None, "head", "seq"),
        ),
        out_specs=P("head", None, "seq"),
        check_vma=False,
    )
```

```python
import functools

import jax
import jax.numpy as jnp
from jax import lax
from jax.experimental import pallas as pl
from jax.experimental.pallas import tpu as pltpu
from jax.sharding import PartitionSpec as P

STRETCH = 64
BLOCK = 256
STEP_BLOCKS = 4
OUT_BLOCKS = 2
HALF = BLOCK // 2
LANES = 128
ROWS = 8
MESH = pl.DeviceIdType.MESH
F32 = jnp.float32
BF16 = jnp.bfloat16


def flip(index, bit):
    return index + bit * (1 - 2 * lax.rem(lax.div(index, bit), 2))


def flip_all(index, mask):
    bit = 1
    while bit <= mask:
        if mask & bit:
            index = flip(index, bit)
        bit *= 2
    return index


def bits_down(count):
    bit = count // 2
    while bit:
        yield bit
        bit //= 2


def scan_kernel(
    head_devices,
    seq_devices,
    v_hbm,
    b_hbm,
    c_hbm,
    ld_hbm,
    w_hbm,
    acc_hbm,
    c_out,
    dev_states,
    dev_offs,
    befores,
    cum_ref,
    v_ref,
    b_all,
    c_all,
    ld_ref,
    w_ref,
    acc,
    steps_ref,
    states,
    lefts,
    tots,
    group,
    send_state,
    send_tot,
    recv_tot,
    local_sem,
    out_sem,
    gather_send,
    gather_recv,
    state_send,
    state_recv,
    tot_send,
    tot_recv,
):
    heads, width, rows = v_hbm.shape
    cols = b_hbm.shape[1]
    blocks = rows // BLOCK
    seq_bits = seq_devices.bit_length() - 1
    me = lax.axis_index("head")
    seq = lax.axis_index("seq")

    load_ld = pltpu.make_async_copy(ld_hbm, ld_ref, local_sem.at[3])
    load_ld.start()
    load_v = pltpu.make_async_copy(v_hbm, v_ref, local_sem.at[0])
    load_v.start()

    partners = [("head", flip(me, bit)) for bit in bits_down(head_devices)]
    partners += [("seq", flip(seq, 2**q)) for q in range(seq_bits)]
    barrier = pltpu.get_barrier_semaphore()
    for axis, who in partners:
        pl.semaphore_signal(barrier, inc=1, device_id={axis: who}, device_id_type=MESH)
    pl.semaphore_wait(barrier, len(partners))

    def slot(full, owner):
        return full.at[:, pl.ds(pl.multiple_of(owner * cols, cols), cols)]

    pairs = ((b_hbm, b_all), (c_hbm, c_all))

    def message(a, mask):
        shard, full = pairs[a]
        bit = mask & -mask
        held = mask ^ bit
        owner = flip_all(me, held)
        return pltpu.make_async_remote_copy(
            src_ref=slot(full, owner) if held else shard,
            dst_ref=slot(full, owner),
            send_sem=gather_send.at[a, mask],
            recv_sem=gather_recv.at[a, mask],
            device_id={"head": flip(me, bit)},
            device_id_type=MESH,
        )

    def send_own(a, least=1):
        for bit in bits_down(head_devices):
            if bit >= least:
                message(a, bit).start()

    def receive(a, mask):
        message(a, mask).wait_recv()
        for lower in bits_down(mask & -mask):
            message(a, mask | lower).start()

    order = [1] if head_devices > 1 else []
    for bit in bits_down(head_devices):
        order += [mask for mask in range(bit, head_devices, 2 * bit) if mask != 1]

    send_own(0)
    if head_devices > 1:
        message(1, 1).start()
    own = []
    for a, (shard, full) in enumerate(pairs):
        copy = pltpu.make_async_copy(shard, slot(full, me), local_sem.at[1 + a])
        copy.start()
        own.append(copy)
    load_w = pltpu.make_async_copy(w_hbm, w_ref, local_sem.at[4])
    load_w.start()

    steps_ref[...] = jnp.zeros_like(steps_ref)
    load_ld.wait()
    for j in range(blocks):
        steps_ref[pl.ds(ROWS * j, heads), :] = ld_ref[:, pl.ds(BLOCK * j, BLOCK)]
    tri = (
        lax.broadcasted_iota(jnp.int32, (BLOCK, BLOCK), 0)
        <= lax.broadcasted_iota(jnp.int32, (BLOCK, BLOCK), 1)
    ).astype(F32)
    cum_ref[...] = jnp.dot(
        steps_ref[...], tri, precision=lax.Precision.HIGHEST, preferred_element_type=F32
    )

    def shard_states(owner):
        per_shard = cols // BLOCK
        for k in range(per_shard):
            j = owner * per_shard + k
            cum = cum_ref[pl.ds(pl.multiple_of(ROWS * j, ROWS), ROWS), :]
            total = cum[:, BLOCK - 1 : BLOCK]
            tots[j] = jnp.broadcast_to(total, (ROWS, LANES))
            fade = jnp.exp(total - cum)
            at = pl.ds(pl.multiple_of(BLOCK * j, BLOCK), BLOCK)
            faded = [
                (v_ref[h, :, at].astype(F32) * fade[h : h + 1, :]).astype(BF16)
                for h in range(heads)
            ]
            states[j] = lax.dot_general(
                jnp.concatenate(faded, axis=0),
                b_all[:, at],
                (((1,), (1,)), ((), ())),
                preferred_element_type=F32,
            )

    inner_bits = STEP_BLOCKS.bit_length() - 1
    step_shards = max(1, STEP_BLOCKS * BLOCK // cols)
    steps = blocks // STEP_BLOCKS

    def merge(base, span, first, count):
        for i in range(count):
            left = (first + i) * (2 * span) + (span - 1)
            right = left + span
            lefts[base + first + i] = states[left].astype(BF16)
            fade = jnp.exp(tots[right])
            for h in range(heads):
                part = pl.ds(h * width, width)
                states[right, part, :] = (
                    fade[h : h + 1, :] * states[left, part, :] + states[right, part, :]
                )
            tots[right] = tots[left] + tots[right]

    def merge_step(step):
        for r in range(inner_bits):
            per_step = STEP_BLOCKS >> (r + 1)
            merge(blocks - (blocks >> r), 2**r, step * per_step, per_step)

    own_step = lax.div(me, step_shards)

    def step_at(i):
        where = own_step
        for bit in bits_down(steps):
            set_here = lax.rem(lax.div(i, bit), 2)
            where = where + set_here * bit * (1 - 2 * lax.rem(lax.div(where, bit), 2))
        return where

    load_v.wait()
    own[0].wait()
    shard_states(me)
    for mask in order:
        if mask < step_shards:
            receive(0, mask)
            shard_states(flip_all(me, mask))
    merge_step(own_step)

    def other_states():
        later = [mask for mask in order if mask >= step_shards]
        sent = False
        for mask in later:
            receive(0, mask)
            if mask != 1 and not sent:
                send_own(1, 2)
                sent = True
            shard_states(flip_all(me, mask))
        if not sent:
            send_own(1, 2)
        for i in range(1, steps):
            merge_step(step_at(i))
        before = jnp.zeros((ROWS, LANES), F32)
        for j in range(blocks):
            cum = cum_ref[ROWS * j : ROWS * (j + 1), :]
            befores[j] = before
            before = before + jnp.broadcast_to(cum[:, BLOCK - 1 : BLOCK], (ROWS, LANES))
        for r in range(inner_bits, blocks.bit_length() - 1):
            merge(blocks - (blocks >> r), 2**r, 0, blocks >> (r + 1))
        last = blocks - 1
        group[...] = states[last]
        send_tot[0] = tots[last]
        dev_offs[0] = jnp.zeros((ROWS, LANES), F32)
        begin(0)

    def swaps(q):
        partner = flip(seq, 2**q)
        return [
            pltpu.make_async_remote_copy(
                src_ref=src.at[q],
                dst_ref=dst.at[q],
                send_sem=send_sem.at[q],
                recv_sem=recv_sem.at[q],
                device_id={"seq": partner},
                device_id_type=MESH,
            )
            for src, dst, send_sem, recv_sem in (
                (send_tot, recv_tot, tot_send, tot_recv),
                (send_state, dev_states, state_send, state_recv),
            )
        ]

    def begin(q):
        send_state[q] = group[...].astype(BF16)
        for copy in swaps(q):
            copy.start()

    def finish(q):
        for copy in swaps(q):
            copy.wait()
        if q < seq_bits - 1:
            right = lax.rem(lax.div(seq, 2**q), 2) == 1
            mine, other = send_tot[q], recv_tot[q]
            mine_by = jnp.where(right, 1.0, jnp.exp(other))
            other_by = jnp.where(right, jnp.exp(mine), 1.0)
            for h in range(heads):
                part = pl.ds(h * width, width)
                group[part, :] = mine_by[h : h + 1, :] * group[part, :] + other_by[
                    h : h + 1, :
                ] * dev_states[q, part, :].astype(F32)
            dev_offs[q + 1] = dev_offs[q] + jnp.where(right, other, 0.0)
            send_tot[q + 1] = mine + other
            begin(q + 1)

    own[1].wait()
    for mask in order:
        if mask < step_shards:
            receive(1, mask)
    load_w.wait()

    local_bits = blocks.bit_length() - 1
    left_base = [blocks - (blocks >> r) for r in range(local_bits)]
    s_at = lax.broadcasted_iota(jnp.int32, (BLOCK, BLOCK), 0)
    t_at = lax.broadcasted_iota(jnp.int32, (BLOCK, BLOCK), 1)
    causal = s_at <= t_at
    near_at = lax.broadcasted_iota(jnp.int32, (heads, BLOCK), 1)
    near = (near_at < STRETCH) | ((near_at >= HALF) & (near_at < HALF + STRETCH))
    empty = jnp.zeros((HALF, HALF), BF16)

    def tokens(j):
        return pl.ds(pl.multiple_of(j * BLOCK, BLOCK), BLOCK)

    def cum_of(j):
        return cum_ref[pl.ds(pl.multiple_of(ROWS * j, ROWS), ROWS), :]

    def level_scale(level, j, off):
        return w_ref[level, :, tokens(j)] * jnp.exp(cum_of(j) + off[:, :1])[:heads]

    def near_levels(step, k):
        j = step * STEP_BLOCKS + k
        at = tokens(j)
        cum = cum_of(j)
        c_blk = c_all[:, at]
        scores = lax.dot_general(
            b_all[:, at], c_blk, (((0,), (0,)), ((), ())), preferred_element_type=F32
        )
        scores = jnp.where(causal, scores, 0.0)
        cut = cum[:, HALF - 1 : HALF]
        col = jnp.exp(cut - cum).T
        row = jnp.exp(cum - cut)[:heads]
        w0, w1, w2 = w_ref[0, :, at], w_ref[1, :, at], w_ref[2, :, at]
        row_first = jnp.where(near, w0, w1) * row
        row_second = w0 * row
        row_cut = w2[:, HALF:] * row[:, HALF:]

        reads = []
        for r in range(inner_bits):
            if k >> r & 1:
                per_step = STEP_BLOCKS >> (r + 1)
                state = lefts[left_base[r] + step * per_step + (k >> (r + 1))]
                off = jnp.zeros((ROWS, 1), F32)
                for i in range(k >> r << r, k):
                    off = off + cum_of(step * STEP_BLOCKS + i)[:, BLOCK - 1 : BLOCK]
                by = level_scale(3 + r, j, off)
                reads.append((jnp.dot(state, c_blk, preferred_element_type=F32), by))

        def piece(h, s0, t0, size, row_part):
            factor = col[s0 : s0 + size, h : h + 1] * row_part[h : h + 1, :]
            return (scores[s0 : s0 + size, t0 : t0 + HALF] * factor).astype(BF16)

        for h in range(heads):
            first = [
                piece(h, 0, 0, STRETCH, row_first[:, :HALF]),
                piece(h, STRETCH, 0, STRETCH, row_second[:, :HALF]),
                empty,
            ]
            second = [
                piece(h, 0, HALF, HALF, row_cut),
                piece(h, HALF, HALF, STRETCH, row_first[:, HALF:]),
                piece(h, HALF + STRETCH, HALF, STRETCH, row_second[:, HALF:]),
            ]
            mix = jnp.concatenate(
                [jnp.concatenate(first, axis=0), jnp.concatenate(second, axis=0)], axis=1
            )
            part = slice(h * width, (h + 1) * width)
            inner = jnp.dot(v_ref[h, :, at], mix, preferred_element_type=F32)
            for read, by in reads:
                inner += read[part, :] * by[h : h + 1, :]
            acc[part, at] = inner

    def add_level(level, step, state, off_of):
        for k in range(STEP_BLOCKS):
            j = step * STEP_BLOCKS + k
            at = tokens(j)
            read = jnp.dot(state, c_all[:, at], preferred_element_type=F32)
            by = level_scale(level, j, off_of(j))
            for h in range(heads):
                part = slice(h * width, (h + 1) * width)
                acc[part, at] += read[part, :] * by[h : h + 1, :]

    shards_of = [
        [mask for mask in order if mask >= step_shards and mask // step_shards == i]
        for i in range(steps)
    ]

    def near_step(i, carry):
        for at in range(1, steps):

            @pl.when(i == at)
            def _(at=at):
                for mask in shards_of[at]:
                    receive(1, mask)

        step = step_at(i)
        for k in range(STEP_BLOCKS):
            near_levels(step, k)
        pl.when(i == 0)(other_states)
        for q in range(min(seq_bits - 1, steps - 2)):
            pl.when(i == q + 1)(functools.partial(finish, q))
        return carry

    lax.fori_loop(0, steps, near_step, 0)
    for q in range(min(seq_bits - 1, steps - 2), seq_bits - 1):
        finish(q)

    def store(step):
        at = pl.ds(pl.multiple_of(step * (STEP_BLOCKS * BLOCK), BLOCK), STEP_BLOCKS * BLOCK)
        return pltpu.make_async_copy(acc.at[:, at], acc_hbm.at[:, at], out_sem.at[step])

    store_c = pltpu.make_async_copy(c_all, c_out, local_sem.at[5])
    store_c.start()

    def far_step(step, carry):
        for r in range(inner_bits, local_bits):
            apart = 2 ** (r - inner_bits)

            @pl.when(lax.rem(lax.div(step, apart), 2) == 1)
            def _(r=r, apart=apart):
                state = lefts[left_base[r] + lax.div(step, 2 * apart)]
                start = lax.div(step, apart) * (apart * STEP_BLOCKS)
                add_level(3 + r, step, state, lambda j: befores[j] - befores[start])

        store(step).start()
        return carry

    lax.fori_loop(0, steps, far_step, 0)
    finish(seq_bits - 1)

    for a in range(2):
        for mask in range(1, head_devices):
            message(a, mask).wait_send()
    for step in range(steps):
        store(step).wait()
    store_c.wait()


def output_kernel(seq_bits, acc_ref, c_ref, dev_states, dev_offs, before_ref, cum_ref, *rest):
    weights, out_ref = rest[:seq_bits], rest[seq_bits]
    heads, width, step = out_ref.shape
    seq = lax.axis_index("seq")
    for k in range(step // BLOCK):
        at = slice(k * BLOCK, (k + 1) * BLOCK)
        cum = cum_ref[ROWS * k : ROWS * (k + 1), :]
        reads = []
        for q in range(seq_bits):
            has = (seq >> q) & 1 == 1
            off = before_ref[k] + dev_offs[q]
            by = weights[q][0, :, at] * jnp.exp(cum + off[:, :1])[:heads]
            read = jnp.dot(dev_states[q], c_ref[:, at], preferred_element_type=F32)
            reads.append((read, jnp.where(has, by, 0.0)))
        for h in range(heads):
            part = slice(h * width, (h + 1) * width)
            total = acc_ref[part, at]
            for read, by in reads:
                total += read[part, :] * by[h : h + 1, :]
            out_ref[h, :, at] = total.astype(BF16)


def on_device(head_devices, seq_devices, values, b_rows, c_rows, log_decay, level_weight):
    heads, width, rows = values.shape
    state_size = b_rows.shape[0]
    blocks = rows // BLOCK
    seq_bits = seq_devices.bit_length() - 1
    hp = heads * width
    hbm = pl.BlockSpec(memory_space=pltpu.HBM)
    dma = pltpu.SemaphoreType.DMA
    vmem = pl.BlockSpec(memory_space=pltpu.VMEM)
    acc, c_all, dev_states, dev_offs, befores, cum = pl.pallas_call(
        functools.partial(scan_kernel, head_devices, seq_devices),
        out_shape=(
            jax.ShapeDtypeStruct((hp, rows), F32),
            jax.ShapeDtypeStruct((state_size, rows), BF16),
            jax.ShapeDtypeStruct((seq_bits, hp, state_size), BF16),
            jax.ShapeDtypeStruct((seq_bits, ROWS, LANES), F32),
            jax.ShapeDtypeStruct((blocks, ROWS, LANES), F32),
            jax.ShapeDtypeStruct((ROWS * blocks, BLOCK), F32),
        ),
        in_specs=[hbm] * 5,
        out_specs=(hbm, hbm, vmem, vmem, vmem, vmem),
        scratch_shapes=[
            pltpu.VMEM(values.shape, BF16),
            pltpu.VMEM((state_size, rows), BF16),
            pltpu.VMEM((state_size, rows), BF16),
            pltpu.VMEM(log_decay.shape, F32),
            pltpu.VMEM(level_weight.shape, F32),
            pltpu.VMEM((hp, rows), F32),
            pltpu.VMEM((ROWS * blocks, BLOCK), F32),
            pltpu.VMEM((blocks, hp, state_size), F32),
            pltpu.VMEM((blocks - 1, hp, state_size), BF16),
            pltpu.VMEM((blocks, ROWS, LANES), F32),
            pltpu.VMEM((hp, state_size), F32),
            pltpu.VMEM((seq_bits, hp, state_size), BF16),
            pltpu.VMEM((seq_bits, ROWS, LANES), F32),
            pltpu.VMEM((seq_bits, ROWS, LANES), F32),
            dma((6,)),
            dma((blocks // STEP_BLOCKS,)),
            dma((2, head_devices)),
            dma((2, head_devices)),
            dma((seq_bits,)),
            dma((seq_bits,)),
            dma((seq_bits,)),
            dma((seq_bits,)),
        ],
        compiler_params=pltpu.CompilerParams(
            collective_id=0, has_side_effects=True, vmem_limit_bytes=60 * 2**20
        ),
        name="scan",
    )(values, b_rows, c_rows, log_decay, level_weight)

    step = OUT_BLOCKS * BLOCK
    first = level_weight.shape[0] - seq_bits
    return pl.pallas_call(
        functools.partial(output_kernel, seq_bits),
        grid=(rows // step,),
        out_shape=jax.ShapeDtypeStruct(values.shape, BF16),
        in_specs=[
            pl.BlockSpec((hp, step), lambda j: (0, j)),
            pl.BlockSpec((state_size, step), lambda j: (0, j)),
            pl.BlockSpec((seq_bits, hp, state_size), lambda j: (0, 0, 0)),
            pl.BlockSpec((seq_bits, ROWS, LANES), lambda j: (0, 0, 0)),
            pl.BlockSpec((OUT_BLOCKS, ROWS, LANES), lambda j: (j, 0, 0)),
            pl.BlockSpec((ROWS * OUT_BLOCKS, BLOCK), lambda j: (j, 0)),
            *(
                pl.BlockSpec((1, heads, step), lambda j, at=first + q: (at, 0, j))
                for q in range(seq_bits)
            ),
        ],
        out_specs=pl.BlockSpec((heads, width, step), lambda j: (0, 0, j)),
        compiler_params=pltpu.CompilerParams(vmem_limit_bytes=60 * 2**20),
        name="outputs",
    )(acc, c_all, dev_states, dev_offs, befores, cum, *([level_weight] * seq_bits))


def solution(mesh):
    return jax.shard_map(
        functools.partial(on_device, mesh.shape["head"], mesh.shape["seq"]),
        mesh=mesh,
        in_specs=(
            P("head", None, "seq"),
            P(None, ("seq", "head")),
            P(None, ("seq", "head")),
            P("head", "seq"),
            P(None, "head", "seq"),
        ),
        out_specs=P("head", None, "seq"),
        check_vma=False,
    )
```
